128 devices in a mesh: owner: 8 (over y_hi, z), dp: 16 (over x, y_lo, core).
Axes of the slice: x: 4, y: 4 (y_hi: 2, y_lo: 2; y = y_hi * 2 + y_lo), z: 4, core: 2. Of those that a mesh axis runs over, the one named last changes fastest.
Arguments:
- query_grad: bfloat16 [1024, 16384], P('dp', 'owner'), may hold values from -6 to 6
- query_act: bfloat16 [1024, 8192], P('dp'), may hold values from -6 to 6
- train_grad: bfloat16 [8192, 16384], P('dp', 'owner'), may hold values from -6 to 6
- train_act: bfloat16 [8192, 8192], P('dp'), may hold values from -6 to 6
- basis_out: bfloat16 [16384, 512], P('owner'), may hold values from -0.25 to 0.25
- basis_in: bfloat16 [8192, 512], P('dp'), may hold values from -0.25 to 0.25
- eigenvalues: float32 [16384, 8192], P('owner', 'dp'), may hold values from 0.1 to 10
Outputs:
- token_scores: float32 [8192], P('dp')
- influence: float32 [128], P('dp')
The draws below stay inside these ranges and needn't reach their ends.
All inputs are finite; a program needn't handle non-finite values.
Results may differ from the reference program's by a relative error of at most 0.0065.
Values may be sent and summed in bfloat16 or wider, within the bound.
A program may use at most 192 MiB of HBM per device.

```python
import math
import jax
import jax.numpy as jnp
from jax import lax

DIN = 8192
DOUT = 16384
EB = 512
SEQ_LEN = 64
QTOK = 1024
TTOK = 8192
SEQS = 128


def block_levels(own_key, shape, cuts, low, largest):
    loudness = 1.0
    for axis_at, blocks in cuts:
        heights = jax.random.uniform(jax.random.fold_in(jax.random.fold_in(own_key, 6), axis_at), (blocks,), jnp.float32, low / len(cuts), largest / len(cuts))
        loudness = loudness * jnp.repeat(jnp.exp(heights), shape[axis_at] // blocks).reshape((-1,) + (1,) * (len(shape) - 1 - axis_at))
    return loudness


def scatter_about(rng, shape, spread, most, split=(), held_as=jnp.bfloat16):
    drawn = spread * jax.random.normal(rng, shape, jnp.float32)
    if split:
        drawn = drawn * block_levels(rng, shape, split, -0.22, 0.18)
    return jnp.clip(drawn, -most, most).astype(held_as)


def setup_inputs(seed: int = 0) -> dict:
    seeds = jax.random.split(jax.random.key(seed), 8)
    query_grad = scatter_about(seeds[0], (QTOK, DOUT), 1.0, 6.0, ((0, 16), (1, 8)))
    query_act = scatter_about(seeds[1], (QTOK, DIN), 1.0, 6.0, ((0, 16),))
    train_grad = scatter_about(seeds[2], (TTOK, DOUT), 1.0, 6.0, ((0, 16), (1, 8)))
    train_act = scatter_about(seeds[3], (TTOK, DIN), 1.0, 6.0, ((0, 16),))
    basis_out = scatter_about(seeds[4], (DOUT, EB), EB ** -0.5, 0.25, ((0, 8),))
    basis_in = scatter_about(seeds[5], (DIN, EB), EB ** -0.5, 0.25, ((0, 16),))
    eigenvalues = jnp.clip(jnp.exp(math.log(10.0) - 4.6051702 * jax.random.uniform(seeds[6], (DOUT, DIN), jnp.float32) ** block_levels(seeds[6], (DOUT, DIN), ((0, 8), (1, 16)), -0.2, 0.2)), 0.1, 10.0)
    return dict(query_grad=query_grad, query_act=query_act, train_grad=train_grad, train_act=train_act, basis_out=basis_out, basis_in=basis_in, eigenvalues=eigenvalues)


def rotate_rows(rows, basis):
    count, width = rows.shape
    size = basis.shape[1]
    parts = rows.astype(jnp.float32).reshape(count, width // size, size)
    blocks = basis.astype(jnp.float32).reshape(width // size, size, size)
    return jnp.einsum('tkr,krc->tkc', parts, blocks).reshape(count, width)

def reference(query_grad, query_act, train_grad, train_act, basis_out, basis_in, eigenvalues):
    grad_rot = rotate_rows(query_grad, basis_out).astype(jnp.bfloat16)
    act_rot = rotate_rows(query_act, basis_in).astype(jnp.bfloat16)
    cross = jnp.dot(grad_rot.T, act_rot, preferred_element_type=jnp.float32)
    scaled = (cross / (math.sqrt(QTOK) * eigenvalues)).astype(jnp.bfloat16)
    out_blocks = basis_out.astype(jnp.float32).reshape(DOUT // EB, EB, EB)
    half = jnp.einsum('krc,kcj->krj', out_blocks, scaled.astype(jnp.float32).reshape(DOUT // EB, EB, DIN))
    half = half.reshape(DOUT, DIN).astype(jnp.bfloat16)
    in_blocks = basis_in.astype(jnp.float32).reshape(DIN // EB, EB, EB)
    precond = jnp.einsum('imc,mjc->imj', half.astype(jnp.float32).reshape(DOUT, DIN // EB, EB), in_blocks)
    precond = precond.reshape(DOUT, DIN).astype(jnp.bfloat16)
    image = lax.dot_general(train_act, precond, (((1,), (1,)), ((), ())), preferred_element_type=jnp.float32)
    token_scores = lax.optimization_barrier(jnp.sum(train_grad.astype(jnp.float32) * image, axis=1)) / math.sqrt(DOUT * DIN)
    influence = lax.optimization_barrier(jnp.mean(token_scores.reshape(SEQS, SEQ_LEN), axis=1))
    return (token_scores, influence)
```

```python
import math

import jax
import jax.numpy as jnp
from jax import lax
from jax.experimental import pallas as pl
from jax.experimental.pallas import tpu as pltpu
from jax.sharding import PartitionSpec as P

DIN = 8192
DOUT = 16384
SEQ_LEN = 64
EB = 512
QTOK = 1024
MESH = pl.DeviceIdType.MESH
F32 = jnp.float32
BF16 = jnp.bfloat16


def mm(a, b, ca=1, cb=0):
    return lax.dot_general(a, b, (((ca,), (cb,)), ((), ())), preferred_element_type=F32)


def kernel(qg, qa, tg, ta, uo, ui, lam, out, qg_v, uo_v, ui_v, lam_v, rlt, gr, ac, art, gb, ab, a_st, pt, acc,
           part, r1, r2, ssem, lsem, ac_s, gr_s, art_s, ab_s, az_s, asib_s, gsem, p_s, r1_s, r2_s):
    dp, ow = lax.axis_index("dp"), lax.axis_index("owner")
    x, yl, c = dp // 4, (dp // 2) % 2, dp % 2
    yh, z = ow // 4, ow % 4
    xr, xl, x2 = (x + 1) % 4, (x + 3) % 4, (x + 2) % 4
    me4 = yl * 2 + c

    def d_of(x_, yl_, c_):
        return (x_ * 2 + yl_) * 2 + c_

    right = (ow, d_of(xr, yl, c))
    left = (ow, d_of(xl, yl, c))
    sib = (ow, d_of(x, yl, 1 - c))
    across = (ow, d_of(x, 1 - yl, c))
    diag = (ow, d_of(x, 1 - yl, 1 - c))
    bnb = ((1 - yh) * 4 + z, d_of(x, 1 - yl, c))
    zs = [(yh * 4 + (z + k) % 4, dp) for k in (1, 3, 2)]
    owners = [((ow + k) % 8, dp) for k in range(1, 8)]
    dps = [(ow, (dp + k) % 16) for k in range(1, 16)]

    bar = pltpu.get_barrier_semaphore()
    peers = dps + owners + [bnb]
    for p in peers:
        pl.semaphore_signal(bar, inc=1, device_id=p, device_id_type=MESH)

    sends, locs = [], []

    def send(src, dst, rsem, to):
        cp = pltpu.make_async_remote_copy(src, dst, ssem.at[len(sends)], rsem, device_id=to, device_id_type=MESH)
        cp.start()
        sends.append(cp)

    def got(region, rsem):
        pltpu.make_async_remote_copy(region, region, ssem.at[0], rsem, device_id=sib, device_id_type=MESH).wait_recv()

    def local(src, dst):
        cp = pltpu.make_async_copy(src, dst, lsem.at[len(locs)])
        cp.start()
        locs.append(cp)
        return cp

    def cols(x_, yl_, c_):
        return pl.ds(pl.multiple_of(x_ * 2048 + yl_ * 1024 + c_ * 512, 512), 512)

    l_qg = local(qg, qg_v)
    l_uo = local(uo, uo_v)
    l_ui = local(ui, ui_v)
    q16 = pl.ds(pl.multiple_of(z * 16, 16), 16)
    l_ac = local(qa.at[q16, pl.ds(pl.multiple_of(dp * 512, 512), 512)], ac.at[dp])
    l_lam = local(lam, lam_v)

    l_qg.wait()
    l_uo.wait()
    for k in range(4):
        rot = mm(qg_v[:, k * 512:(k + 1) * 512], uo_v[k * 512:(k + 1) * 512, :])
        gr[k, :, dp, :, :] = rot.astype(BF16).reshape(4, 16, 512)

    pl.semaphore_wait(bar, len(peers))

    for to in dps:
        send(qa.at[q16, pl.ds(pl.multiple_of(to[1] * 512, 512), 512)], ac.at[dp], ac_s, to)

    def gblock(d, h):
        return gr.at[pl.ds(2 * h, 2), :, d]

    def gsend(d, h, to):
        send(gblock(d, h), gblock(d, h), gr_s.at[d, h], to)

    def ggot(d, h):
        got(gblock(d, h), gr_s.at[d, h])

    for h in range(2):
        for to in (right, left, across, sib):
            gsend(dp, h, to)

    z128 = pl.ds(pl.multiple_of(z * 128, 128), 128)
    for k in range(4):
        at = slice(k * 512, (k + 1) * 512)
        send(ta.at[z128, cols(k, 1 - yl, 1 - c)], a_st.at[:, at], ab_s.at[1], bnb)
    for k in range(4):
        at = slice(k * 512, (k + 1) * 512)
        send(ta.at[z128, cols(k, 1 - yl, c)], ab.at[me4, z128, at], ab_s.at[0], bnb)

    def recip(k):
        rlt[k] = (1.0 / (math.sqrt(QTOK) * lam_v[k * 512:(k + 1) * 512, :])).T

    l_lam.wait()
    recip(0)

    l_ui.wait()
    l_ac.wait()
    got(ac.at[pl.ds(0, 15)], ac_s)
    art[z] = mm(ac[...].reshape(256, 512), ui_v[...]).T.astype(BF16)
    for to in zs:
        send(art.at[z], art.at[z], art_s.at[z], to)

    dl, dr, da = d_of(xl, yl, c), d_of(xr, yl, c), d_of(x, 1 - yl, c)
    for h in range(2):
        ggot(da, h)
        gsend(da, h, right)
        gsend(da, h, left)
        ggot(dl, h)
        if h == 0:
            gsend(dl, h, right)
        ggot(dr, h)
        if h == 1:
            gsend(dr, h, left)
        for d in (da, dl, dr):
            gsend(d, h, sib)
    recip(1)
    for h in range(2):
        d2 = d_of(x2, yl, c)
        ggot(d2, h)
        gsend(d2, h, across)
        gsend(d2, h, sib)
    for h in range(2):
        for x_ in (xl, xr):
            d = d_of(x_, 1 - yl, c)
            ggot(d, h)
            gsend(d, h, sib)
    for h in range(2):
        d = d_of(x2, 1 - yl, c)
        ggot(d, h)
        gsend(d, h, sib)

    send(tg, gb.at[me4], gsem.at[me4], across)
    send(tg, gb.at[me4], gsem.at[me4], sib)
    for k in range(4):
        send(ta.at[:, cols(k, yl, 1 - c)], ab.at[me4, :, k * 512:(k + 1) * 512], asib_s.at[0], sib)
    l_g = local(tg, gb.at[me4])
    l_a = [local(ta.at[:, cols(k, yl, c)], ab.at[me4, :, k * 512:(k + 1) * 512]) for k in range(4)]

    s_ac, s_ad = (1 - yl) * 2 + c, (1 - yl) * 2 + 1 - c
    got(a_st, ab_s.at[1])
    send(a_st, ab.at[s_ac, z128], asib_s.at[1], sib)
    got(ab.at[s_ac, z128], ab_s.at[0])
    for to in zs:
        send(ab.at[s_ac, z128], ab.at[s_ac, z128], az_s.at[0, z], to)
    got(ab.at[s_ad, z128], asib_s.at[1])
    for to in zs:
        send(ab.at[s_ad, z128], ab.at[s_ad, z128], az_s.at[1, z], to)

    recip(2)
    recip(3)
    for k in (1, 2, 3):
        z_ = (z + k) % 4
        got(art.at[z_], art_s.at[z_])

    def xrows(x_):
        return pl.ds(pl.multiple_of(x_ * 512, 512), 512)

    for k in range(4):
        if k % 2 == 0:
            for x_ in range(4):
                for y_ in range(2):
                    ggot(d_of(x_, y_, 1 - c), k // 2)
        cross = mm(art[0], gr[k, 0].reshape(256, 512))
        for z_ in range(1, 4):
            cross = cross + mm(art[z_], gr[k, z_].reshape(256, 512))
        scaled = (cross * rlt[k]).astype(BF16)
        half = mm(scaled, uo_v[k * 512:(k + 1) * 512, :], 1, 1).astype(BF16)
        pt[k, xrows(x), :] = mm(ui_v[...], half).astype(BF16)
        mine = pt.at[k, xrows(x)]
        send(mine, mine, p_s.at[k, 0], right)
        send(mine, mine, p_s.at[k, 1], left)

    acc[...] = jnp.zeros_like(acc)

    def image(k, tb):
        @pl.loop(0, 2)
        def _(r):
            rows = pl.ds(pl.multiple_of(r * 256, 256), 256)
            img = mm(ab[tb, rows, :], pt[k])
            prod = img * gb[tb, rows, k * 512:(k + 1) * 512].astype(F32)
            acc[tb, rows, :] += prod[:, :128] + prod[:, 128:256] + prod[:, 256:384] + prod[:, 384:]

    def relay(k):
        from_l = pt.at[k, xrows(xl)]
        got(from_l, p_s.at[k, 0])
        half0 = pt.at[k, pl.ds(pl.multiple_of(xl * 512, 512), 256)]
        send(half0, half0, p_s.at[k, 2], right)
        from_r = pt.at[k, xrows(xr)]
        got(from_r, p_s.at[k, 1])
        half1 = pt.at[k, pl.ds(pl.multiple_of(xr * 512 + 256, 256), 256)]
        send(half1, half1, p_s.at[k, 3], left)

    def p_all(k):
        got(pt.at[k, pl.ds(pl.multiple_of(x2 * 512, 512), 256)], p_s.at[k, 2])
        got(pt.at[k, pl.ds(pl.multiple_of(x2 * 512 + 256, 256), 256)], p_s.at[k, 3])

    relay(0)
    l_g.wait()
    for cp in l_a:
        cp.wait()
    got(gb.at[me4 + 1 - 2 * c], gsem.at[me4 + 1 - 2 * c])
    got(ab.at[me4 + 1 - 2 * c], asib_s.at[0])
    tb_own, tb_sib = me4, me4 + 1 - 2 * c
    relay(1)
    p_all(0)
    image(0, tb_own)
    image(0, tb_sib)
    relay(2)
    got(gb.at[s_ac], gsem.at[s_ac])
    send(gb.at[s_ac], gb.at[s_ac], gsem.at[s_ac], sib)
    p_all(1)
    image(1, tb_own)
    image(1, tb_sib)
    for k in (1, 2, 3):
        z_ = (z + k) % 4
        rows = pl.ds(pl.multiple_of(z_ * 128, 128), 128)
        got(ab.at[s_ac, rows], az_s.at[0, z_])
        got(ab.at[s_ad, rows], az_s.at[1, z_])
    got(gb.at[s_ad], gsem.at[s_ad])
    relay(3)
    for k in range(2):
        image(k, s_ac)
        image(k, s_ad)
    for k in range(2, 4):
        p_all(k)
        for tb in (tb_own, tb_sib, s_ac, s_ad):
            image(k, tb)

    for tb in range(4):
        part[tb] = jnp.sum(acc[tb].T, axis=0, keepdims=True)
    for to, slot in ((sib, tb_sib), (across, s_ac), (diag, s_ad)):
        send(part.at[slot], r1.at[me4], r1_s.at[me4], to)
    r1[me4] = part[me4]
    for slot in (tb_sib, s_ac, s_ad):
        got(r1.at[slot], r1_s.at[slot])
    r2[ow] = (r1[0] + r1[1]) + (r1[2] + r1[3])
    for to in owners:
        send(r2.at[ow], r2.at[ow], r2_s.at[ow], to)
    for o in owners:
        got(r2.at[o[0]], r2_s.at[o[0]])
    total = r2[0]
    for o in range(1, 8):
        total = total + r2[o]
    out[...] = total * (1.0 / math.sqrt(DOUT * DIN))
    for cp in sends:
        cp.wait_send()


def on_device(query_grad, query_act, train_grad, train_act, basis_out, basis_in, eigenvalues):
    dma, vmem = pltpu.SemaphoreType.DMA, pltpu.VMEM
    scores = pl.pallas_call(
        kernel,
        out_shape=jax.ShapeDtypeStruct((1, 512), F32),
        in_specs=[pl.BlockSpec(memory_space=pl.ANY)] * 7,
        out_specs=pl.BlockSpec(memory_space=pltpu.VMEM),
        scratch_shapes=[
            vmem((64, 2048), BF16),
            vmem((2048, 512), BF16),
            vmem((512, 512), BF16),
            vmem((2048, 512), F32),
            vmem((4, 512, 512), F32),
            vmem((4, 4, 16, 16, 512), BF16),
            vmem((16, 16, 512), BF16),
            vmem((4, 512, 256), BF16),
            vmem((4, 512, 2048), BF16),
            vmem((4, 512, 2048), BF16),
            vmem((128, 2048), BF16),
            vmem((4, 2048, 512), BF16),
            vmem((4, 512, 128), F32),
            vmem((4, 1, 512), F32),
            vmem((4, 1, 512), F32),
            vmem((8, 1, 512), F32),
            dma((100,)),
            dma((12,)),
            dma,
            dma((16, 2)),
            dma((4,)),
            dma((2,)),
            dma((2, 4)),
            dma((2,)),
            dma((4,)),
            dma((4, 4)),
            dma((4,)),
            dma((8,)),
        ],
        compiler_params=pltpu.CompilerParams(
            collective_id=0, has_side_effects=True, vmem_limit_bytes=60 * 2**20
        ),
        cost_estimate=pl.CostEstimate(flops=22 * 10**9, bytes_accessed=18 * 2**20, transcendentals=0),
        name="influence",
    )(query_grad, query_act, train_grad, train_act, basis_out, basis_in, eigenvalues)
    token_scores = scores.reshape(512)
    influence = jnp.mean(token_scores.reshape(512 // SEQ_LEN, SEQ_LEN), axis=1)
    return (token_scores, influence)


def solution(mesh):
    placed = (
        P("dp", "owner"),
        P("dp", None),
        P("dp", "owner"),
        P("dp", None),
        P("owner", None),
        P("dp", None),
        P("owner", "dp"),
    )
    return jax.shard_map(
        on_device, mesh=mesh, in_specs=placed, out_specs=(P("dp"), P("dp")), check_vma=False
    )
```

```python
import math

import jax
import jax.numpy as jnp
from jax import lax
from jax.experimental import pallas as pl
from jax.experimental.pallas import tpu as pltpu
from jax.sharding import PartitionSpec as P

DIN = 8192
DOUT = 16384
SEQ_LEN = 64
EB = 512
QTOK = 1024
MESH = pl.DeviceIdType.MESH
F32 = jnp.float32
BF16 = jnp.bfloat16


def mm(a, b, ca=1, cb=0):
    return lax.dot_general(a, b, (((ca,), (cb,)), ((), ())), preferred_element_type=F32)


def kernel(qg, qa, tg, ta, uo, ui, lam, out, out2, qg_v, uo_v, ui_v, lam_v, rlt, gr, ac, art, gb, ab, a_st, pt, acc,
           part, r1, r2, ssem, lsem, ac_s, gr_s, art_s, ab_s, az_s, asib_s, gsem, p_s, r1_s, r2_s):
    dp, ow = lax.axis_index("dp"), lax.axis_index("owner")
    x, yl, c = dp // 4, (dp // 2) % 2, dp % 2
    yh, z = ow // 4, ow % 4
    xr, xl, x2 = (x + 1) % 4, (x + 3) % 4, (x + 2) % 4
    me4 = yl * 2 + c

    def d_of(x_, yl_, c_):
        return (x_ * 2 + yl_) * 2 + c_

    right = (ow, d_of(xr, yl, c))
    left = (ow, d_of(xl, yl, c))
    sib = (ow, d_of(x, yl, 1 - c))
    across = (ow, d_of(x, 1 - yl, c))
    diag = (ow, d_of(x, 1 - yl, 1 - c))
    bnb = ((1 - yh) * 4 + z, d_of(x, 1 - yl, c))
    zs = [(yh * 4 + (z + k) % 4, dp) for k in (1, 3, 2)]
    owners = [((ow + k) % 8, dp) for k in range(1, 8)]
    dps = [(ow, (dp + k) % 16) for k in range(1, 16)]

    bar = pltpu.get_barrier_semaphore()
    peers = dps + owners + [bnb]
    for p in peers:
        pl.semaphore_signal(bar, inc=1, device_id=p, device_id_type=MESH)

    sends, locs = [], []

    def send(src, dst, rsem, to):
        cp = pltpu.make_async_remote_copy(src, dst, ssem.at[len(sends)], rsem, device_id=to, device_id_type=MESH)
        cp.start()
        sends.append(cp)

    def got(region, rsem):
        pltpu.make_async_remote_copy(region, region, ssem.at[0], rsem, device_id=sib, device_id_type=MESH).wait_recv()

    def local(src, dst):
        cp = pltpu.make_async_copy(src, dst, lsem.at[len(locs)])
        cp.start()
        locs.append(cp)
        return cp

    def cols(x_, yl_, c_):
        return pl.ds(pl.multiple_of(x_ * 2048 + yl_ * 1024 + c_ * 512, 512), 512)

    xs = (x, xl, xr, x2)

    l_qg = local(qg, qg_v)
    l_uo = local(uo, uo_v)
    l_ui = local(ui, ui_v)
    q16 = pl.ds(pl.multiple_of(z * 16, 16), 16)
    l_ac = local(qa.at[q16, pl.ds(pl.multiple_of(dp * 512, 512), 512)], ac.at[dp])
    l_lam = local(lam, lam_v)

    l_qg.wait()
    l_uo.wait()
    for k in range(4):
        rot = mm(qg_v[:, k * 512:(k + 1) * 512], uo_v[k * 512:(k + 1) * 512, :])
        gr[k, :, dp, :, :] = rot.astype(BF16).reshape(4, 16, 512)

    pl.semaphore_wait(bar, len(peers))

    for to in dps:
        send(qa.at[q16, pl.ds(pl.multiple_of(to[1] * 512, 512), 512)], ac.at[dp], ac_s, to)

    def gblock(d, h):
        return gr.at[pl.ds(2 * h, 2), :, d]

    def gsend(d, h, to):
        send(gblock(d, h), gblock(d, h), gr_s.at[d, h], to)

    def ggot(d, h):
        got(gblock(d, h), gr_s.at[d, h])

    for h in range(2):
        for to in (right, left, across, sib):
            gsend(dp, h, to)

    z128 = pl.ds(pl.multiple_of(z * 128, 128), 128)
    for k in range(4):
        at = slice(k * 512, (k + 1) * 512)
        send(ta.at[z128, cols(xs[k], 1 - yl, 1 - c)], a_st.at[:, at], ab_s.at[1], bnb)
    for k in range(4):
        at = slice(k * 512, (k + 1) * 512)
        send(ta.at[z128, cols(xs[k], 1 - yl, c)], ab.at[me4, z128, at], ab_s.at[0], bnb)

    def recip(k):
        rlt[k] = (1.0 / (math.sqrt(QTOK) * lam_v[k * 512:(k + 1) * 512, :])).T

    l_lam.wait()
    recip(0)

    l_ui.wait()
    l_ac.wait()
    got(ac.at[pl.ds(0, 15)], ac_s)
    art[z] = mm(ac[...].reshape(256, 512), ui_v[...]).T.astype(BF16)
    for to in zs:
        send(art.at[z], art.at[z], art_s.at[z], to)

    dl, dr, da = d_of(xl, yl, c), d_of(xr, yl, c), d_of(x, 1 - yl, c)
    d2, dl_a, dr_a, d2_a = d_of(x2, yl, c), d_of(xl, 1 - yl, c), d_of(xr, 1 - yl, c), d_of(x2, 1 - yl, c)

    def near(h):
        ggot(da, h)
        gsend(da, h, right)
        gsend(da, h, left)
        ggot(dl, h)
        if h == 0:
            gsend(dl, h, right)
        ggot(dr, h)
        if h == 1:
            gsend(dr, h, left)
        for d in (da, dl, dr):
            gsend(d, h, sib)

    def far(h):
        ggot(d2, h)
        gsend(d2, h, across)
        gsend(d2, h, sib)

    def rest(h):
        for d in (dl_a, dr_a, d2_a):
            ggot(d, h)
            gsend(d, h, sib)

    near(0)
    near(1)
    far(0)
    recip(1)
    far(1)
    rest(0)

    send(tg, gb.at[me4], gsem.at[me4], across)
    send(tg, gb.at[me4], gsem.at[me4], sib)
    for k in range(4):
        send(ta.at[:, cols(xs[k], yl, 1 - c)], ab.at[me4, :, k * 512:(k + 1) * 512], asib_s.at[0], sib)
    l_g = local(tg, gb.at[me4])
    l_a = [local(ta.at[:, cols(xs[k], yl, c)], ab.at[me4, :, k * 512:(k + 1) * 512]) for k in range(4)]

    def pre(k):
        cross = mm(art[0], gr[k, 0].reshape(256, 512))
        for z_ in range(1, 4):
            cross = cross + mm(art[z_], gr[k, z_].reshape(256, 512))
        scaled = (cross * rlt[k]).astype(BF16)
        half = mm(scaled, uo_v[k * 512:(k + 1) * 512, :], 1, 1).astype(BF16)
        pt[k, :512, :] = mm(ui_v[...], half).astype(BF16)

    def psend(k):
        send(pt.at[k, :512], pt.at[k, 512:1024], p_s.at[k, 0], right)
        send(pt.at[k, :512], pt.at[k, 1024:1536], p_s.at[k, 1], left)

    def sibs(h):
        for x_ in range(4):
            for y_ in range(2):
                ggot(d_of(x_, y_, 1 - c), h)

    for k in (1, 2, 3):
        z_ = (z + k) % 4
        got(art.at[z_], art_s.at[z_])
    sibs(0)
    pre(0)
    psend(0)
    rest(1)
    pre(1)
    psend(1)

    s_ac, s_ad = (1 - yl) * 2 + c, (1 - yl) * 2 + 1 - c
    got(a_st, ab_s.at[1])
    send(a_st, ab.at[s_ac, z128], asib_s.at[1], sib)
    recip(2)
    recip(3)
    sibs(1)
    pre(2)
    pre(3)
    got(ab.at[s_ac, z128], ab_s.at[0])
    for to in zs:
        send(ab.at[s_ac, z128], ab.at[s_ac, z128], az_s.at[0, z], to)
    got(ab.at[s_ad, z128], asib_s.at[1])
    for to in zs:
        send(ab.at[s_ad, z128], ab.at[s_ad, z128], az_s.at[1, z], to)

    acc[...] = jnp.zeros_like(acc)

    def image(k, tb, lo, hi):
        @pl.loop(0, 2)
        def _(r):
            rows = pl.ds(pl.multiple_of(r * 256, 256), 256)
            img = mm(ab[tb, rows, lo:hi], pt[k, lo:hi, :])
            prod = img * gb[tb, rows, k * 512:(k + 1) * 512].astype(F32)
            acc[tb, rows, :] += prod[:, :128] + prod[:, 128:256] + prod[:, 256:384] + prod[:, 384:]

    def relay(k):
        got(pt.at[k, 512:1024], p_s.at[k, 0])
        send(pt.at[k, 512:768], pt.at[k, 1536:1792], p_s.at[k, 2], right)
        got(pt.at[k, 1024:1536], p_s.at[k, 1])
        send(pt.at[k, 1280:1536], pt.at[k, 1792:2048], p_s.at[k, 3], left)

    def p_all(k):
        got(pt.at[k, 1536:1792], p_s.at[k, 2])
        got(pt.at[k, 1792:2048], p_s.at[k, 3])

    tb_own, tb_sib = me4, me4 + 1 - 2 * c
    here, there = (tb_sib, tb_own), (s_ad, s_ac)
    near3, far1, full = (0, 1536), (1536, 2048), (0, 2048)

    def images(k, tbs, span):
        for tb in tbs:
            image(k, tb, *span)

    relay(0)
    psend(2)
    l_g.wait()
    for cp in l_a:
        cp.wait()
    got(gb.at[tb_sib], gsem.at[tb_sib])
    got(ab.at[tb_sib], asib_s.at[0])
    images(0, here, near3)
    relay(1)
    psend(3)
    images(1, here, near3)
    p_all(0)
    images(0, here, far1)
    relay(2)
    got(gb.at[s_ac], gsem.at[s_ac])
    send(gb.at[s_ac], gb.at[s_ac], gsem.at[s_ac], sib)
    images(2, here, near3)
    p_all(1)
    images(1, here, far1)
    for k in (1, 2, 3):
        z_ = (z + k) % 4
        rows = pl.ds(pl.multiple_of(z_ * 128, 128), 128)
        got(ab.at[s_ac, rows], az_s.at[0, z_])
        got(ab.at[s_ad, rows], az_s.at[1, z_])
    got(gb.at[s_ad], gsem.at[s_ad])
    images(0, there, full)
    images(1, there, full)
    images(2, there, near3)
    relay(3)
    images(3, there + here, near3)
    p_all(2)
    images(2, there + here, far1)
    p_all(3)

    for slot, to in ((s_ad, diag), (s_ac, across), (tb_sib, sib), (tb_own, None)):
        image(3, slot, *far1)
        if to is None:
            r1[slot] = jnp.sum(acc[slot].T, axis=0, keepdims=True)
        else:
            part[slot] = jnp.sum(acc[slot].T, axis=0, keepdims=True)
            send(part.at[slot], r1.at[me4], r1_s.at[me4], to)
    for slot in (s_ad, s_ac, tb_sib):
        got(r1.at[slot], r1_s.at[slot])
    r2[ow] = (r1[0] + r1[1]) + (r1[2] + r1[3])
    for to in owners:
        send(r2.at[ow], r2.at[ow], r2_s.at[ow], to)
    for o in owners:
        got(r2.at[o[0]], r2_s.at[o[0]])
    total = r2[0]
    for o in range(1, 8):
        total = total + r2[o]
    total = total * (1.0 / math.sqrt(DOUT * DIN))
    out[...] = total.reshape(512)
    token = lax.broadcasted_iota(jnp.int32, (512, 128), 0) // SEQ_LEN
    spread = jnp.where(token == lax.broadcasted_iota(jnp.int32, (512, 128), 1), 1.0 / SEQ_LEN, 0.0).astype(F32)
    means = lax.dot_general(total, spread, (((1,), (0,)), ((), ())), precision=lax.Precision.HIGHEST, preferred_element_type=F32)
    out2[...] = means.reshape(128)[:8]
    for cp in sends:
        cp.wait_send()


def on_device(query_grad, query_act, train_grad, train_act, basis_out, basis_in, eigenvalues):
    dma, vmem = pltpu.SemaphoreType.DMA, pltpu.VMEM
    return pl.pallas_call(
        kernel,
        out_shape=(jax.ShapeDtypeStruct((512,), F32), jax.ShapeDtypeStruct((8,), F32)),
        in_specs=[pl.BlockSpec(memory_space=pl.ANY)] * 7,
        out_specs=(pl.BlockSpec(memory_space=pltpu.VMEM),) * 2,
        scratch_shapes=[
            vmem((64, 2048), BF16),
            vmem((2048, 512), BF16),
            vmem((512, 512), BF16),
            vmem((2048, 512), F32),
            vmem((4, 512, 512), F32),
            vmem((4, 4, 16, 16, 512), BF16),
            vmem((16, 16, 512), BF16),
            vmem((4, 512, 256), BF16),
            vmem((4, 512, 2048), BF16),
            vmem((4, 512, 2048), BF16),
            vmem((128, 2048), BF16),
            vmem((4, 2048, 512), BF16),
            vmem((4, 512, 128), F32),
            vmem((4, 1, 512), F32),
            vmem((4, 1, 512), F32),
            vmem((8, 1, 512), F32),
            dma((100,)),
            dma((12,)),
            dma,
            dma((16, 2)),
            dma((4,)),
            dma((2,)),
            dma((2, 4)),
            dma((2,)),
            dma((4,)),
            dma((4, 4)),
            dma((4,)),
            dma((8,)),
        ],
        compiler_params=pltpu.CompilerParams(
            collective_id=0, has_side_effects=True, vmem_limit_bytes=60 * 2**20
        ),
        cost_estimate=pl.CostEstimate(flops=22 * 10**9, bytes_accessed=18 * 2**20, transcendentals=0),
        name="influence",
    )(query_grad, query_act, train_grad, train_act, basis_out, basis_in, eigenvalues)


def solution(mesh):
    placed = (
        P("dp", "owner"),
        P("dp", None),
        P("dp", "owner"),
        P("dp", None),
        P("owner", None),
        P("dp", None),
        P("owner", "dp"),
    )
    return jax.shard_map(
        on_device, mesh=mesh, in_specs=placed, out_specs=(P("dp"), P("dp")), check_vma=False
    )
```

```python
import math

import jax
import jax.numpy as jnp
from jax import lax
from jax.experimental import pallas as pl
from jax.experimental.pallas import tpu as pltpu
from jax.sharding import PartitionSpec as P

DIN = 8192
DOUT = 16384
SEQ_LEN = 64
EB = 512
QTOK = 1024
MESH = pl.DeviceIdType.MESH
F32 = jnp.float32
BF16 = jnp.bfloat16


def mm(a, b, ca=1, cb=0):
    return lax.dot_general(a, b, (((ca,), (cb,)), ((), ())), preferred_element_type=F32)


def kernel(qg, qa, tg, ta, uo, ui, lam, out, out2, qa_v, qg_v, uo_v, ui_v, lam_v, rlt, gr, ac, art, gb, ab, a_st, pt, acc,
           part, r1, r2, ssem, lsem, ac_s, gr_s, art_s, ab_s, az_s, asib_s, gsem, p_s, r1_s, r2_s):
    dp, ow = lax.axis_index("dp"), lax.axis_index("owner")
    x, yl, c = dp // 4, (dp // 2) % 2, dp % 2
    yh, z = ow // 4, ow % 4
    xr, xl, x2 = (x + 1) % 4, (x + 3) % 4, (x + 2) % 4
    me4 = yl * 2 + c

    def d_of(x_, yl_, c_):
        return (x_ * 2 + yl_) * 2 + c_

    right = (ow, d_of(xr, yl, c))
    left = (ow, d_of(xl, yl, c))
    sib = (ow, d_of(x, yl, 1 - c))
    across = (ow, d_of(x, 1 - yl, c))
    diag = (ow, d_of(x, 1 - yl, 1 - c))
    bnb = ((1 - yh) * 4 + z, d_of(x, 1 - yl, c))
    zs = [(yh * 4 + (z + k) % 4, dp) for k in (1, 3, 2)]
    owners = [((ow + k) % 8, dp) for k in range(1, 8)]
    dps = [(ow, (dp + k) % 16) for k in range(1, 16)]

    bar = pltpu.get_barrier_semaphore()
    peers = dps + owners + [bnb]
    for p in peers:
        pl.semaphore_signal(bar, inc=1, device_id=p, device_id_type=MESH)

    sends, locs = [], []

    def send(src, dst, rsem, to):
        cp = pltpu.make_async_remote_copy(src, dst, ssem.at[len(sends)], rsem, device_id=to, device_id_type=MESH)
        cp.start()
        sends.append(cp)

    def got(region, rsem):
        pltpu.make_async_remote_copy(region, region, ssem.at[0], rsem, device_id=sib, device_id_type=MESH).wait_recv()

    def local(src, dst):
        cp = pltpu.make_async_copy(src, dst, lsem.at[len(locs)])
        cp.start()
        locs.append(cp)
        return cp

    def cols(x_, yl_, c_):
        return pl.ds(pl.multiple_of(x_ * 2048 + yl_ * 1024 + c_ * 512, 512), 512)

    xs = (x, xl, xr, x2)

    l_qg = local(qg, qg_v)
    l_uo = local(uo, uo_v)
    l_ui = local(ui, ui_v)
    q16 = pl.ds(pl.multiple_of(z * 16, 16), 16)
    l_qa = local(qa.at[q16], qa_v)
    l_lam = local(lam, lam_v)

    l_qa.wait()
    pl.semaphore_wait(bar, len(peers))

    def feats(d):
        return pl.ds(pl.multiple_of(d * 512, 512), 512)

    for to in dps:
        send(qa_v.at[:, feats(to[1])], ac.at[dp], ac_s, to)

    def gblock(d, h, part=None):
        units = pl.ds(h, 1 + h // 2)
        if part is None:
            return gr.at[units, :, d]
        return gr.at[units, :, d, :, part * 256:(part + 1) * 256]

    def gsend(d, h, to, part=None):
        send(gblock(d, h, part), gblock(d, h, part), gr_s.at[d, h, part or 0], to)

    def ggot(d, h, part=None):
        got(gblock(d, h, part), gr_s.at[d, h, part or 0])

    l_qg.wait()
    l_uo.wait()

    def rotate(k):
        rot = mm(qg_v[:, k * 512:(k + 1) * 512], uo_v[k * 512:(k + 1) * 512, :])
        gr[k, :, dp, :, :] = rot.astype(BF16).reshape(4, 16, 512)

    for h in range(3):
        rotate(h)
        if h == 2:
            rotate(3)
        for to in (right, left, across, sib):
            gsend(dp, h, to)
    ac[dp] = qa_v[:, feats(dp)]

    z128 = pl.ds(pl.multiple_of(z * 128, 128), 128)
    for k in range(4):
        at = slice(k * 512, (k + 1) * 512)
        send(ta.at[z128, cols(xs[k], 1 - yl, c)], ab.at[me4, z128, at], ab_s.at[0], bnb)

    def recip(k):
        rlt[k] = (1.0 / (math.sqrt(QTOK) * lam_v[k * 512:(k + 1) * 512, :])).T


    l_ui.wait()
    got(ac.at[pl.ds(0, 15)], ac_s)
    art[z] = mm(ac[...].reshape(256, 512), ui_v[...]).T.astype(BF16)
    z_up, z_down, z_far = (z + 1) % 4, (z + 3) % 4, (z + 2) % 4
    up, down = (yh * 4 + z_up, dp), (yh * 4 + z_down, dp)

    def asend(z_, part, to):
        rows = slice(part * 256, (part + 1) * 256)
        send(art.at[z_, rows], art.at[z_, rows], art_s.at[z_, part], to)

    def agot(z_, part):
        got(art.at[z_, part * 256:(part + 1) * 256], art_s.at[z_, part])

    asend(z, 0, up)
    asend(z, 1, down)
    asend(z, 1, up)
    asend(z, 0, down)

    dl, dr, da = d_of(xl, yl, c), d_of(xr, yl, c), d_of(x, 1 - yl, c)
    d2, dl_a, dr_a, d2_a = d_of(x2, yl, c), d_of(xl, 1 - yl, c), d_of(xr, 1 - yl, c), d_of(x2, 1 - yl, c)

    def ring(h):
        ggot(dl, h)
        gsend(dl, h, right, 0)
        ggot(dr, h)
        gsend(dr, h, left, 1)
        for d in (dl, dr):
            gsend(d, h, across)
            gsend(d, h, sib)

    ring(0)
    l_lam.wait()
    recip(0)
    agot(z_down, 0)
    asend(z_down, 0, up)
    agot(z_up, 1)
    asend(z_up, 1, down)

    def far(h):
        ggot(d2, h, 0)
        ggot(d2, h, 1)
        gsend(d2, h, across)
        gsend(d2, h, sib)

    def rest(h):
        for d in (da, dl_a, dr_a, d2_a):
            ggot(d, h)
            gsend(d, h, sib)

    far(0)
    ring(1)
    for k in range(4):
        at = slice(k * 512, (k + 1) * 512)
        send(ta.at[z128, cols(xs[k], 1 - yl, 1 - c)], a_st.at[:, at], ab_s.at[1], bnb)
    rest(0)
    ring(2)
    recip(1)

    def pre(k):
        cross = mm(art[0], gr[k, 0].reshape(256, 512))
        for z_ in range(1, 4):
            cross = cross + mm(art[z_], gr[k, z_].reshape(256, 512))
        scaled = (cross * rlt[k]).astype(BF16)
        half = mm(scaled, uo_v[k * 512:(k + 1) * 512, :], 1, 1).astype(BF16)
        pt[k, :512, :] = mm(ui_v[...], half).astype(BF16)

    def psend(k):
        send(pt.at[k, :512], pt.at[k, 512:1024], p_s.at[k, 0], right)
        send(pt.at[k, :512], pt.at[k, 1024:1536], p_s.at[k, 1], left)

    def sibs(h):
        for x_ in range(4):
            for y_ in range(2):
                ggot(d_of(x_, y_, 1 - c), h)

    agot(z_down, 1)
    agot(z_up, 0)
    agot(z_far, 0)
    agot(z_far, 1)
    sibs(0)
    pre(0)
    psend(0)

    s_ac, s_ad = (1 - yl) * 2 + c, (1 - yl) * 2 + 1 - c
    tb_own, tb_sib = me4, me4 + 1 - 2 * c

    def a_along_z(slot, which):
        for to in zs:
            send(ab.at[slot, z128], ab.at[slot, z128], az_s.at[which, z], to)

    far(1)
    far(2)
    for k in range(4):
        at = slice(k * 512, (k + 1) * 512)
        send(tg.at[:, at], gb.at[me4, :, at], gsem.at[me4, k], across)
    got(ab.at[s_ac, z128], ab_s.at[0])
    a_along_z(s_ac, 0)
    for k in range(4):
        at = slice(k * 512, (k + 1) * 512)
        send(tg.at[:, at], gb.at[me4, :, at], gsem.at[me4, k], sib)
    for k in range(4):
        send(ta.at[:, cols(xs[k], yl, 1 - c)], ab.at[me4, :, k * 512:(k + 1) * 512], asib_s.at[0], sib)
    l_g = local(tg, gb.at[me4])
    l_a = [local(ta.at[:, cols(xs[k], yl, c)], ab.at[me4, :, k * 512:(k + 1) * 512]) for k in range(4)]

    def g_pass(k):
        at = slice(k * 512, (k + 1) * 512)
        got(gb.at[s_ac, :, at], gsem.at[s_ac, k])
        send(gb.at[s_ac, :, at], gb.at[s_ac, :, at], gsem.at[s_ac, k], sib)

    def g_got(slot, k):
        got(gb.at[slot, :, k * 512:(k + 1) * 512], gsem.at[slot, k])

    rest(1)
    sibs(1)
    pre(1)
    psend(1)
    got(a_st, ab_s.at[1])
    send(a_st, ab.at[s_ac, z128], asib_s.at[1], sib)
    recip(2)
    recip(3)
    rest(2)
    sibs(2)
    pre(2)
    pre(3)
    got(ab.at[s_ad, z128], asib_s.at[1])
    a_along_z(s_ad, 1)

    acc[...] = jnp.zeros_like(acc)

    def image(k, tb, lo, hi):
        @pl.loop(0, 2)
        def _(r):
            rows = pl.ds(pl.multiple_of(r * 256, 256), 256)
            img = mm(ab[tb, rows, lo:hi], pt[k, lo:hi, :])
            prod = img * gb[tb, rows, k * 512:(k + 1) * 512].astype(F32)
            acc[tb, rows, :] += prod[:, :128] + prod[:, 128:256] + prod[:, 256:384] + prod[:, 384:]

    def relay(k):
        got(pt.at[k, 512:1024], p_s.at[k, 0])
        send(pt.at[k, 512:768], pt.at[k, 1536:1792], p_s.at[k, 2], right)
        got(pt.at[k, 1024:1536], p_s.at[k, 1])
        send(pt.at[k, 1280:1536], pt.at[k, 1792:2048], p_s.at[k, 3], left)

    def p_all(k):
        got(pt.at[k, 1536:1792], p_s.at[k, 2])
        got(pt.at[k, 1792:2048], p_s.at[k, 3])

    here, there = (tb_sib, tb_own), (s_ad, s_ac)
    near3, far1, full = (0, 1536), (1536, 2048), (0, 2048)

    def images(k, tbs, span):
        for tb in tbs:
            image(k, tb, *span)

    relay(0)
    psend(2)
    l_g.wait()
    for cp in l_a:
        cp.wait()
    for k in range(4):
        g_got(tb_sib, k)
    got(ab.at[tb_sib], asib_s.at[0])
    images(0, here, near3)
    relay(1)
    psend(3)
    g_pass(0)
    images(1, here, near3)
    p_all(0)
    images(0, here, far1)
    g_pass(1)
    relay(2)
    images(2, here, near3)
    p_all(1)
    images(1, here, far1)
    for k in (1, 2, 3):
        z_ = (z + k) % 4
        rows = pl.ds(pl.multiple_of(z_ * 128, 128), 128)
        got(ab.at[s_ac, rows], az_s.at[0, z_])
        got(ab.at[s_ad, rows], az_s.at[1, z_])
    g_pass(2)
    g_got(s_ad, 0)
    images(0, there, full)
    g_pass(3)
    relay(3)
    g_got(s_ad, 1)
    images(1, there, full)
    g_got(s_ad, 2)
    images(2, there, near3)
    p_all(2)
    images(2, here + there, far1)
    g_got(s_ad, 3)
    images(3, there + here, near3)
    p_all(3)

    for slot, to in ((s_ad, diag), (s_ac, across), (tb_sib, sib), (tb_own, None)):
        image(3, slot, *far1)
        if to is None:
            r1[slot] = jnp.sum(acc[slot].T, axis=0, keepdims=True)
        else:
            part[slot] = jnp.sum(acc[slot].T, axis=0, keepdims=True)
            send(part.at[slot], r1.at[me4], r1_s.at[me4], to)
    for slot in (s_ad, s_ac, tb_sib):
        got(r1.at[slot], r1_s.at[slot])
    r2[ow] = (r1[0] + r1[1]) + (r1[2] + r1[3])
    for to in owners:
        send(r2.at[ow], r2.at[ow], r2_s.at[ow], to)
    for o in owners:
        got(r2.at[o[0]], r2_s.at[o[0]])
    total = r2[0]
    for o in range(1, 8):
        total = total + r2[o]
    total = total * (1.0 / math.sqrt(DOUT * DIN))
    out[...] = total.reshape(512)
    token = lax.broadcasted_iota(jnp.int32, (512, 128), 0) // SEQ_LEN
    spread = jnp.where(token == lax.broadcasted_iota(jnp.int32, (512, 128), 1), 1.0 / SEQ_LEN, 0.0).astype(F32)
    means = lax.dot_general(total, spread, (((1,), (0,)), ((), ())), precision=lax.Precision.HIGHEST, preferred_element_type=F32)
    out2[...] = means.reshape(128)[:8]
    for cp in sends:
        cp.wait_send()


def on_device(query_grad, query_act, train_grad, train_act, basis_out, basis_in, eigenvalues):
    dma, vmem = pltpu.SemaphoreType.DMA, pltpu.VMEM
    return pl.pallas_call(
        kernel,
        out_shape=(jax.ShapeDtypeStruct((512,), F32), jax.ShapeDtypeStruct((8,), F32)),
        in_specs=[pl.BlockSpec(memory_space=pl.ANY)] * 7,
        out_specs=(pl.BlockSpec(memory_space=pltpu.VMEM),) * 2,
        scratch_shapes=[
            vmem((16, 8192), BF16),
            vmem((64, 2048), BF16),
            vmem((2048, 512), BF16),
            vmem((512, 512), BF16),
            vmem((2048, 512), F32),
            vmem((4, 512, 512), F32),
            vmem((4, 4, 16, 16, 512), BF16),
            vmem((16, 16, 512), BF16),
            vmem((4, 512, 256), BF16),
            vmem((4, 512, 2048), BF16),
            vmem((4, 512, 2048), BF16),
            vmem((128, 2048), BF16),
            vmem((4, 2048, 512), BF16),
            vmem((4, 512, 128), F32),
            vmem((4, 1, 512), F32),
            vmem((4, 1, 512), F32),
            vmem((8, 1, 512), F32),
            dma((140,)),
            dma((12,)),
            dma,
            dma((16, 3, 2)),
            dma((4, 2)),
            dma((2,)),
            dma((2, 4)),
            dma((2,)),
            dma((4, 4)),
            dma((4, 4)),
            dma((4,)),
            dma((8,)),
        ],
        compiler_params=pltpu.CompilerParams(
            collective_id=0, has_side_effects=True, vmem_limit_bytes=60 * 2**20
        ),
        cost_estimate=pl.CostEstimate(flops=22 * 10**9, bytes_accessed=18 * 2**20, transcendentals=0),
        name="influence",
    )(query_grad, query_act, train_grad, train_act, basis_out, basis_in, eigenvalues)


def solution(mesh):
    placed = (
        P("dp", "owner"),
        P("dp", None),
        P("dp", "owner"),
        P("dp", None),
        P("owner", None),
        P("dp", None),
        P("owner", "dp"),
    )
    return jax.shard_map(
        on_device, mesh=mesh, in_specs=placed, out_specs=(P("dp"), P("dp")), check_vma=False
    )
```

```python
import math

import jax
import jax.numpy as jnp
from jax import lax
from jax.experimental import pallas as pl
from jax.experimental.pallas import tpu as pltpu
from jax.sharding import PartitionSpec as P

DIN = 8192
DOUT = 16384
SEQ_LEN = 64
EB = 512
QTOK = 1024
MESH = pl.DeviceIdType.MESH
F32 = jnp.float32
BF16 = jnp.bfloat16


def mm(a, b, ca=1, cb=0):
    return lax.dot_general(a, b, (((ca,), (cb,)), ((), ())), preferred_element_type=F32)


def kernel(qg, qa, tg, ta, uo, ui, lam, out, out2, qa_v, qg_v, uo_v, ui_v, lam_v, rlt, gr, ac, art, gb, ab, a_st, pt, acc,
           part, r1, r2, ssem, lsem, ac_s, gr_s, art_s, ab_s, az_s, asib_s, gsem, p_s, r1_s, r2_s):
    dp, ow = lax.axis_index("dp"), lax.axis_index("owner")
    x, yl, c = dp // 4, (dp // 2) % 2, dp % 2
    yh, z = ow // 4, ow % 4
    xr, xl, x2 = (x + 1) % 4, (x + 3) % 4, (x + 2) % 4
    me4 = yl * 2 + c

    def d_of(x_, yl_, c_):
        return (x_ * 2 + yl_) * 2 + c_

    right = (ow, d_of(xr, yl, c))
    left = (ow, d_of(xl, yl, c))
    sib = (ow, d_of(x, yl, 1 - c))
    across = (ow, d_of(x, 1 - yl, c))
    diag = (ow, d_of(x, 1 - yl, 1 - c))
    bnb = ((1 - yh) * 4 + z, d_of(x, 1 - yl, c))
    zs = [(yh * 4 + (z + k) % 4, dp) for k in (1, 3, 2)]
    owners = [((ow + k) % 8, dp) for k in range(1, 8)]
    dps = [(ow, (dp + k) % 16) for k in range(1, 16)]

    bar = pltpu.get_barrier_semaphore()
    peers = dps + owners + [bnb]
    for p in peers:
        pl.semaphore_signal(bar, inc=1, device_id=p, device_id_type=MESH)

    sends, locs = [], []

    def send(src, dst, rsem, to):
        cp = pltpu.make_async_remote_copy(src, dst, ssem.at[len(sends)], rsem, device_id=to, device_id_type=MESH)
        cp.start()
        sends.append(cp)

    def got(region, rsem):
        pltpu.make_async_remote_copy(region, region, ssem.at[0], rsem, device_id=sib, device_id_type=MESH).wait_recv()

    def local(src, dst):
        cp = pltpu.make_async_copy(src, dst, lsem.at[len(locs)])
        cp.start()
        locs.append(cp)
        return cp

    def cols(x_, yl_, c_):
        return pl.ds(pl.multiple_of(x_ * 2048 + yl_ * 1024 + c_ * 512, 512), 512)

    xs = (x, xl, xr, x2)

    l_qg = local(qg, qg_v)
    l_uo = local(uo, uo_v)
    l_ui = local(ui, ui_v)
    q16 = pl.ds(pl.multiple_of(z * 16, 16), 16)
    l_qa = local(qa.at[q16], qa_v)
    l_lam = local(lam, lam_v)

    l_qa.wait()
    pl.semaphore_wait(bar, len(peers))

    def feats(d):
        return pl.ds(pl.multiple_of(d * 512, 512), 512)

    for to in dps:
        send(qa_v.at[:, feats(to[1])], ac.at[dp], ac_s, to)

    def gblock(d, h, part=None):
        units = pl.ds(h, 1 + h // 2)
        if part is None:
            return gr.at[units, :, d]
        return gr.at[units, :, d, :, part * 256:(part + 1) * 256]

    def gsend(d, h, to, part=None):
        send(gblock(d, h, part), gblock(d, h, part), gr_s.at[d, h, part or 0], to)

    def ggot(d, h, part=None):
        got(gblock(d, h, part), gr_s.at[d, h, part or 0])

    l_qg.wait()
    l_uo.wait()

    def rotate(k):
        rot = mm(qg_v[:, k * 512:(k + 1) * 512], uo_v[k * 512:(k + 1) * 512, :])
        gr[k, :, dp, :, :] = rot.astype(BF16).reshape(4, 16, 512)

    for h in range(3):
        rotate(h)
        if h == 2:
            rotate(3)
        for to in (right, left, across, sib):
            gsend(dp, h, to)
    ac[dp] = qa_v[:, feats(dp)]

    z128 = pl.ds(pl.multiple_of(z * 128, 128), 128)
    for k in range(4):
        at = slice(k * 512, (k + 1) * 512)
        send(ta.at[z128, cols(xs[k], 1 - yl, c)], ab.at[me4, z128, at], ab_s.at[0], bnb)

    def recip(k):
        rlt[k] = (1.0 / (math.sqrt(QTOK) * lam_v[k * 512:(k + 1) * 512, :])).T


    l_ui.wait()
    got(ac.at[pl.ds(0, 15)], ac_s)
    art[z] = mm(ac[...].reshape(256, 512), ui_v[...]).T.astype(BF16)
    z_up, z_down, z_far = (z + 1) % 4, (z + 3) % 4, (z + 2) % 4
    up, down = (yh * 4 + z_up, dp), (yh * 4 + z_down, dp)

    def asend(z_, part, to):
        rows = slice(part * 256, (part + 1) * 256)
        send(art.at[z_, rows], art.at[z_, rows], art_s.at[z_, part], to)

    def agot(z_, part):
        got(art.at[z_, part * 256:(part + 1) * 256], art_s.at[z_, part])

    asend(z, 0, up)
    asend(z, 1, down)
    asend(z, 1, up)
    asend(z, 0, down)

    dl, dr, da = d_of(xl, yl, c), d_of(xr, yl, c), d_of(x, 1 - yl, c)
    d2, dl_a, dr_a, d2_a = d_of(x2, yl, c), d_of(xl, 1 - yl, c), d_of(xr, 1 - yl, c), d_of(x2, 1 - yl, c)

    def ring(h):
        ggot(dl, h)
        gsend(dl, h, right, 0)
        ggot(dr, h)
        gsend(dr, h, left, 1)
        for d in (dl, dr):
            gsend(d, h, across)
            gsend(d, h, sib)

    ring(0)
    l_lam.wait()
    recip(0)
    agot(z_down, 0)
    asend(z_down, 0, up)
    agot(z_up, 1)
    asend(z_up, 1, down)

    def far(h):
        ggot(d2, h, 0)
        ggot(d2, h, 1)
        gsend(d2, h, across)
        gsend(d2, h, sib)

    def rest(h):
        for d in (da, dl_a, dr_a, d2_a):
            ggot(d, h)
            gsend(d, h, sib)

    far(0)
    ring(1)
    for k in range(4):
        at = slice(k * 512, (k + 1) * 512)
        send(ta.at[z128, cols(xs[k], 1 - yl, 1 - c)], a_st.at[:, at], ab_s.at[1], bnb)
    rest(0)
    ring(2)
    recip(1)

    def pre(k):
        cross = mm(art[0], gr[k, 0].reshape(256, 512))
        for z_ in range(1, 4):
            cross = cross + mm(art[z_], gr[k, z_].reshape(256, 512))
        scaled = (cross * rlt[k]).astype(BF16)
        half = mm(scaled, uo_v[k * 512:(k + 1) * 512, :], 1, 1).astype(BF16)
        pt[k, :512, :] = mm(ui_v[...], half).astype(BF16)

    def psend(k):
        send(pt.at[k, :512], pt.at[k, 512:1024], p_s.at[k, 0], right)
        send(pt.at[k, :512], pt.at[k, 1024:1536], p_s.at[k, 1], left)

    def sibs(h):
        for x_ in range(4):
            for y_ in range(2):
                ggot(d_of(x_, y_, 1 - c), h)

    agot(z_down, 1)
    agot(z_up, 0)
    agot(z_far, 0)
    agot(z_far, 1)
    sibs(0)
    pre(0)
    psend(0)

    s_ac, s_ad = (1 - yl) * 2 + c, (1 - yl) * 2 + 1 - c
    tb_own, tb_sib = me4, me4 + 1 - 2 * c

    def a_along_z(slot, which):
        for to in zs:
            send(ab.at[slot, z128], ab.at[slot, z128], az_s.at[which, z], to)

    far(1)
    far(2)
    for k in range(4):
        at = slice(k * 512, (k + 1) * 512)
        send(tg.at[:, at], gb.at[me4, :, at], gsem.at[me4, k], across)
    got(ab.at[s_ac, z128], ab_s.at[0])
    a_along_z(s_ac, 0)
    for k in range(4):
        at = slice(k * 512, (k + 1) * 512)
        send(tg.at[:, at], gb.at[me4, :, at], gsem.at[me4, k], sib)
    for k in range(4):
        send(ta.at[:, cols(xs[k], yl, 1 - c)], ab.at[me4, :, k * 512:(k + 1) * 512], asib_s.at[0], sib)
    l_g = local(tg, gb.at[me4])
    l_a = [local(ta.at[:, cols(xs[k], yl, c)], ab.at[me4, :, k * 512:(k + 1) * 512]) for k in range(4)]

    def g_pass(k):
        at = slice(k * 512, (k + 1) * 512)
        got(gb.at[s_ac, :, at], gsem.at[s_ac, k])
        send(gb.at[s_ac, :, at], gb.at[s_ac, :, at], gsem.at[s_ac, k], sib)

    def g_got(slot, k):
        got(gb.at[slot, :, k * 512:(k + 1) * 512], gsem.at[slot, k])

    rest(1)
    sibs(1)
    pre(1)
    psend(1)
    got(a_st, ab_s.at[1])
    send(a_st, ab.at[s_ac, z128], asib_s.at[1], sib)
    recip(2)
    recip(3)
    rest(2)
    sibs(2)
    pre(2)
    pre(3)
    got(ab.at[s_ad, z128], asib_s.at[1])
    a_along_z(s_ad, 1)

    acc[...] = jnp.zeros_like(acc)

    def image(k, tb, lo, hi):
        @pl.loop(0, 2)
        def _(r):
            rows = pl.ds(pl.multiple_of(r * 256, 256), 256)
            img = mm(ab[tb, rows, lo:hi], pt[k, lo:hi, :])
            prod = img * gb[tb, rows, k * 512:(k + 1) * 512].astype(F32)
            acc[tb, rows, :] += prod[:, :128] + prod[:, 128:256] + prod[:, 256:384] + prod[:, 384:]

    def relay(k):
        got(pt.at[k, 512:1024], p_s.at[k, 0])
        send(pt.at[k, 512:768], pt.at[k, 1536:1792], p_s.at[k, 2], right)
        got(pt.at[k, 1024:1536], p_s.at[k, 1])
        send(pt.at[k, 1280:1536], pt.at[k, 1792:2048], p_s.at[k, 3], left)

    def p_all(k):
        got(pt.at[k, 1536:1792], p_s.at[k, 2])
        got(pt.at[k, 1792:2048], p_s.at[k, 3])

    here, there = (tb_sib, tb_own), (s_ad, s_ac)
    near3, far1, full = (0, 1536), (1536, 2048), (0, 2048)

    def images(k, tbs, span):
        for tb in tbs:
            image(k, tb, *span)

    relay(0)
    psend(2)
    l_g.wait()
    for cp in l_a:
        cp.wait()
    for k in range(4):
        g_got(tb_sib, k)
    got(ab.at[tb_sib], asib_s.at[0])
    images(0, here, near3)
    relay(1)
    psend(3)
    g_pass(0)
    images(1, here, near3)
    p_all(0)
    images(0, here, far1)
    g_pass(1)
    relay(2)
    images(2, here, near3)
    p_all(1)
    images(1, here, far1)
    for k in (1, 2, 3):
        z_ = (z + k) % 4
        rows = pl.ds(pl.multiple_of(z_ * 128, 128), 128)
        got(ab.at[s_ac, rows], az_s.at[0, z_])
        got(ab.at[s_ad, rows], az_s.at[1, z_])
    g_pass(2)
    g_got(s_ad, 0)
    images(0, there, full)
    g_got(s_ad, 1)
    images(1, there, full)
    relay(3)
    g_pass(3)
    g_got(s_ad, 2)
    images(2, there, near3)
    images(3, here, near3)
    g_got(s_ad, 3)
    images(3, there, near3)
    p_all(2)
    images(2, here + there, far1)
    p_all(3)

    for slot, to in ((s_ad, diag), (s_ac, across), (tb_sib, sib), (tb_own, None)):
        image(3, slot, *far1)
        if to is None:
            r1[slot] = jnp.sum(acc[slot].T, axis=0, keepdims=True)
        else:
            part[slot] = jnp.sum(acc[slot].T, axis=0, keepdims=True)
            send(part.at[slot], r1.at[me4], r1_s.at[me4], to)
    for slot in (s_ad, s_ac, tb_sib):
        got(r1.at[slot], r1_s.at[slot])
    r2[ow] = (r1[0] + r1[1]) + (r1[2] + r1[3])
    for to in owners:
        send(r2.at[ow], r2.at[ow], r2_s.at[ow], to)
    for o in owners:
        got(r2.at[o[0]], r2_s.at[o[0]])
    total = r2[0]
    for o in range(1, 8):
        total = total + r2[o]
    total = total * (1.0 / math.sqrt(DOUT * DIN))
    out[...] = total.reshape(512)
    token = lax.broadcasted_iota(jnp.int32, (512, 128), 0) // SEQ_LEN
    spread = jnp.where(token == lax.broadcasted_iota(jnp.int32, (512, 128), 1), 1.0 / SEQ_LEN, 0.0).astype(F32)
    means = lax.dot_general(total, spread, (((1,), (0,)), ((), ())), precision=lax.Precision.HIGHEST, preferred_element_type=F32)
    out2[...] = means.reshape(128)[:8]
    for cp in sends:
        cp.wait_send()


def on_device(query_grad, query_act, train_grad, train_act, basis_out, basis_in, eigenvalues):
    dma, vmem = pltpu.SemaphoreType.DMA, pltpu.VMEM
    return pl.pallas_call(
        kernel,
        out_shape=(jax.ShapeDtypeStruct((512,), F32), jax.ShapeDtypeStruct((8,), F32)),
        in_specs=[pl.BlockSpec(memory_space=pl.ANY)] * 7,
        out_specs=(pl.BlockSpec(memory_space=pltpu.VMEM),) * 2,
        scratch_shapes=[
            vmem((16, 8192), BF16),
            vmem((64, 2048), BF16),
            vmem((2048, 512), BF16),
            vmem((512, 512), BF16),
            vmem((2048, 512), F32),
            vmem((4, 512, 512), F32),
            vmem((4, 4, 16, 16, 512), BF16),
            vmem((16, 16, 512), BF16),
            vmem((4, 512, 256), BF16),
            vmem((4, 512, 2048), BF16),
            vmem((4, 512, 2048), BF16),
            vmem((128, 2048), BF16),
            vmem((4, 2048, 512), BF16),
            vmem((4, 512, 128), F32),
            vmem((4, 1, 512), F32),
            vmem((4, 1, 512), F32),
            vmem((8, 1, 512), F32),
            dma((140,)),
            dma((12,)),
            dma,
            dma((16, 3, 2)),
            dma((4, 2)),
            dma((2,)),
            dma((2, 4)),
            dma((2,)),
            dma((4, 4)),
            dma((4, 4)),
            dma((4,)),
            dma((8,)),
        ],
        compiler_params=pltpu.CompilerParams(
            collective_id=0, has_side_effects=True, vmem_limit_bytes=60 * 2**20
        ),
        cost_estimate=pl.CostEstimate(flops=22 * 10**9, bytes_accessed=18 * 2**20, transcendentals=0),
        name="influence",
    )(query_grad, query_act, train_grad, train_act, basis_out, basis_in, eigenvalues)


def solution(mesh):
    placed = (
        P("dp", "owner"),
        P("dp", None),
        P("dp", "owner"),
        P("dp", None),
        P("owner", None),
        P("dp", None),
        P("owner", "dp"),
    )
    return jax.shard_map(
        on_device, mesh=mesh, in_specs=placed, out_specs=(P("dp"), P("dp")), check_vma=False
    )
```
